32 devices in a mesh: lat: 4 (over z), lon: 8 (over y, x, core).
Axes of the slice: x: 2, y: 2, z: 4, core: 2. Of those that a mesh axis runs over, the one named last changes fastest.
Arguments:
- grid_input: bfloat16 [65536, 227], P(('lat', 'lon')), may hold values from -6 to 6
- mesh_input: bfloat16 [32768, 512], P(('lat', 'lon')), may hold values from -6 to 6
- cotangent: bfloat16 [32768, 512], P(('lat', 'lon')), may hold values from -0.078125 to 0.078125
- embed_weight: bfloat16 [227, 512], replicated, may hold values from -0.375 to 0.375
- enc_sender: bfloat16 [512, 512], replicated, may hold values from -0.25 to 0.25
- enc_receiver: bfloat16 [512, 512], replicated, may hold values from -0.25 to 0.25
- enc_update: bfloat16 [512, 512], replicated, may hold values from -0.25 to 0.25
- proc_sender: bfloat16 [512, 512], replicated, may hold values from -0.25 to 0.25
- proc_receiver: bfloat16 [512, 512], replicated, may hold values from -0.25 to 0.25
- proc_update: bfloat16 [512, 512], replicated, may hold values from -0.25 to 0.25
- grid_slots: int32 [16384], P(('lat', 'lon')), may hold values from 0 to 2047
- enc_edges: int32 [6, 32768], P(None, ('lat', 'lon')), may hold values from 0 to 2559, as said below
- mesh_slots: int32 [16384], P(('lat', 'lon')), may hold values from 0 to 1023
- mesh_edges: int32 [6, 32768], P(None, ('lat', 'lon')), may hold values from 0 to 1535, as said below
Outputs:
- mesh_out: bfloat16 [32768, 512], P(('lat', 'lon'))
- grad_embed: float32 [227, 512], replicated
- grad_enc_sender: float32 [512, 512], replicated
- grad_enc_receiver: float32 [512, 512], replicated
- grad_enc_update: float32 [512, 512], replicated
- grad_proc_sender: float32 [512, 512], replicated
- grad_proc_receiver: float32 [512, 512], replicated
- grad_proc_update: float32 [512, 512], replicated
The draws below stay inside these ranges and needn't reach their ends.
Inputs may be any that keep to these rules, and one draw needn't show every extreme that they name: `enc_edges`: an entry below 2048 names a grid row of the receiver's own tile; any other entry names slot c of code q as in the reference program. No entry names a neighbour beyond the first or last latitude band. `mesh_edges`: an entry below 1024 names a mesh row of the receiver's own partition; any other entry names slot c of code q as in the reference program. No entry names a neighbour beyond the first or last latitude band.
All inputs are finite; a program needn't handle non-finite values.
Results may differ from the reference program's by a relative error of at most 0.012.
Values may be sent and summed in bfloat16 or wider, within the bound.
A program may use at most 128 MiB of HBM per device.

```python
import jax
import jax.numpy as jnp
from jax import lax

H = 512
GF = 227
G_DEV = 2048
M_DEV = 1024
K_ENC = 6
K_MESH = 6
CAP = 64
GRID = 65536
MESH = 32768
SLOTS = 16384
N_LAT = 4
N_LON = 8


def edge_entries(key, own_rows, receivers, fan_count):
    subkeys = jax.random.split(key, 4)
    node_total = N_LAT * N_LON * receivers
    draw_shape = (fan_count, node_total)
    local_rows = jax.random.randint(subkeys[0], draw_shape, 0, own_rows)
    offset_codes = jax.random.randint(subkeys[1], draw_shape, 0, 8)
    slot_index = jax.random.randint(subkeys[2], draw_shape, 0, CAP)
    remote = jax.random.randint(subkeys[3], draw_shape, 0, 4) == 0
    lat_band = jnp.arange(node_total, dtype=jnp.int32) // receivers // N_LON
    blocked = (offset_codes <= 2) & (lat_band == 0) | (offset_codes >= 5) & (lat_band == N_LAT - 1)
    offset_codes = jnp.where(blocked, 7 - offset_codes, offset_codes)
    entries = jnp.where(remote, own_rows + offset_codes * CAP + slot_index, local_rows)
    entries = entries.at[0, 0].set(own_rows + 8 * CAP - 1)
    entries = entries.at[0, 1].set(0)
    return entries.astype(jnp.int32)


def draw_enc_edges(key, part):
    key = jax.random.fold_in(key, 11)
    return edge_entries(key, G_DEV, M_DEV, K_ENC)


def draw_mesh_edges(key, part):
    key = jax.random.fold_in(key, 12)
    return edge_entries(key, M_DEV, M_DEV, K_MESH)


def plant(values, stream_key, smallest, largest):
    shape = values.shape
    spot = [jax.random.randint(jax.random.fold_in(stream_key, axis), (), 0, shape[axis]) for axis in range(len(shape))]
    values = values.at[tuple(spot)].set(smallest)
    longest = shape.index(max(shape))
    spot[longest] = (spot[longest] + 1) % shape[longest]
    return values.at[tuple(spot)].set(largest)


def level_of(rng, shape, cuts, low, high):
    def one(axis_at, blocks):
        heights = jax.random.uniform(jax.random.fold_in(jax.random.fold_in(rng, 6), axis_at), (blocks,), jnp.float32, low / len(cuts), high / len(cuts))
        return jnp.repeat(jnp.exp(heights), shape[axis_at] // blocks).reshape((-1,) + (1,) * (len(shape) - axis_at - 1))

    loudness = one(*cuts[0])
    for cut in cuts[1:]:
        loudness = loudness * one(*cut)
    return loudness


def centred(rng, shape, deviation, bound, cuts=(), kind=jnp.bfloat16):
    values = deviation * jax.random.normal(rng, shape, jnp.float32)
    if cuts:
        values = values * level_of(rng, shape, cuts, -0.22, 0.18)
    return jnp.clip(values, -bound, bound).astype(kind)


def setup_inputs(seed: int = 0) -> dict:
    keys = jax.random.split(jax.random.key(seed), 15)
    grid_input = centred(keys[0], (GRID, GF), 1.0, 6.0, ((0, 32),))
    mesh_input = centred(keys[1], (MESH, H), 1.0, 6.0, ((0, 32),))
    cotangent = centred(keys[2], (MESH, H), (MESH ** -0.5), 0.078125, ((0, 32),))
    embed_weight = centred(keys[3], (GF, H), GF ** -0.5, 0.375)
    enc_sender = centred(keys[4], (H, H), H ** -0.5, 0.25)
    enc_receiver = centred(keys[5], (H, H), H ** -0.5, 0.25)
    enc_update = centred(keys[6], (H, H), H ** -0.5, 0.25)
    proc_sender = centred(keys[7], (H, H), H ** -0.5, 0.25)
    proc_receiver = centred(keys[8], (H, H), H ** -0.5, 0.25)
    proc_update = centred(keys[9], (H, H), H ** -0.5, 0.25)
    grid_slots = plant(jax.random.randint(keys[10], (SLOTS,), 0, G_DEV), jax.random.fold_in(keys[10], 1), 0, G_DEV - 1).astype(jnp.int32)
    enc_edges = draw_enc_edges(jax.random.fold_in(keys[14], 71), 0)
    mesh_slots = plant(jax.random.randint(keys[12], (SLOTS,), 0, M_DEV), jax.random.fold_in(keys[12], 1), 0, M_DEV - 1).astype(jnp.int32)
    mesh_edges = draw_mesh_edges(jax.random.fold_in(keys[14], 71), 0)
    return {"grid_input": grid_input, "mesh_input": mesh_input, "cotangent": cotangent, "embed_weight": embed_weight, "enc_sender": enc_sender, "enc_receiver": enc_receiver, "enc_update": enc_update, "proc_sender": proc_sender, "proc_receiver": proc_receiver, "proc_update": proc_update, "grid_slots": grid_slots, "enc_edges": enc_edges, "mesh_slots": mesh_slots, "mesh_edges": mesh_edges}


lat_steps = (-1, -1, -1, 0, 0, 1, 1, 1)
lon_steps = (-1, 0, 1, -1, 1, -1, 0, 1)


def silu_slope(values):
    sigmoid = jax.nn.sigmoid(values)
    return sigmoid * (1.0 + values * (1.0 - sigmoid))


def transpose_dot(left, right):
    return lax.dot_general(left, right, (((0,), (0,)), ((), ())), preferred_element_type=jnp.float32)


def dot_transposed(left, right):
    return lax.dot_general(left, right, (((1,), (1,)), ((), ())), preferred_element_type=jnp.float32)


def global_sources(sources, send_table, own_rows, receivers):
    receiver = (jnp.arange(sources.shape[1], dtype=jnp.int32) // receivers)[None, :]
    receiver = jnp.broadcast_to(receiver, sources.shape)
    is_local = sources < own_rows
    offset_slot = jnp.maximum(sources - own_rows, 0)
    offset_code = offset_slot // CAP
    slot_index = offset_slot % CAP
    lat_table = jnp.array(lat_steps, jnp.int32)
    lon_table = jnp.array(lon_steps, jnp.int32)
    source_lat = jnp.clip(receiver // N_LON + lat_table[offset_code], 0, N_LAT - 1)
    source_lon = (receiver % N_LON + lon_table[offset_code]) % N_LON
    source_device = source_lat * N_LON + source_lon
    sent_row = send_table[(source_device * 8 + 7 - offset_code) * CAP + slot_index]
    return jnp.where(is_local, receiver * own_rows + sources, source_device * own_rows + sent_row).astype(jnp.int32)


def split_blocks(indices, receiver_rows):
    fan_count = indices.shape[0]
    device_count = N_LAT * N_LON
    blocks = indices.reshape(fan_count, device_count, -1).transpose(1, 0, 2)
    recv_blocks = receiver_rows.reshape(device_count, -1, receiver_rows.shape[1])
    return blocks, recv_blocks


def edge_sums(sender_rows, receiver_rows, indices):
    blocks, recv_blocks = split_blocks(indices, receiver_rows)

    def one_block(paired):
        block_ids, block_recv = paired
        before = sender_rows[block_ids].astype(jnp.float32) + block_recv[None]
        return jnp.sum(jax.nn.silu(before), axis=0)

    sums = lax.map(one_block, (blocks, recv_blocks))
    return sums.reshape(receiver_rows.shape)


def edge_grads(sender_rows, receiver_rows, indices, grad_rows):
    blocks, recv_blocks = split_blocks(indices, receiver_rows)
    grad_blocks = grad_rows.reshape(recv_blocks.shape)
    feature_width = receiver_rows.shape[1]

    def one_block(carry, triple):
        block_ids, block_recv, block_grad = triple
        before = sender_rows[block_ids].astype(jnp.float32) + block_recv[None]
        edge_grad = block_grad[None] * silu_slope(before)
        carry = carry.at[block_ids.reshape(-1)].add(edge_grad.reshape(-1, feature_width))
        return carry, jnp.sum(edge_grad, axis=0)

    start = jnp.zeros((sender_rows.shape[0], feature_width), jnp.float32)
    sender_grad, recv_grad = lax.scan(one_block, start, (blocks, recv_blocks, grad_blocks))
    return recv_grad.reshape(receiver_rows.shape), sender_grad


def reference(grid_input, mesh_input, cotangent, embed_weight, enc_sender, enc_receiver, enc_update, proc_sender, proc_receiver, proc_update, grid_slots, enc_edges, mesh_slots, mesh_edges):
    enc_source = global_sources(enc_edges, grid_slots, G_DEV, M_DEV)
    proc_source = global_sources(mesh_edges, mesh_slots, M_DEV, M_DEV)
    pre_grid = jnp.dot(grid_input, embed_weight, preferred_element_type=jnp.float32)
    grid_latent = jax.nn.silu(pre_grid).astype(jnp.bfloat16)
    enc_message = jnp.dot(grid_latent, enc_sender, preferred_element_type=jnp.float32).astype(jnp.bfloat16)
    enc_target = jnp.dot(mesh_input, enc_receiver, preferred_element_type=jnp.float32)
    enc_sum = edge_sums(enc_message, enc_target, enc_source).astype(jnp.bfloat16)
    mesh_mid = (mesh_input.astype(jnp.float32) + jnp.dot(enc_sum, enc_update, preferred_element_type=jnp.float32)).astype(jnp.bfloat16)
    proc_message = jnp.dot(mesh_mid, proc_sender, preferred_element_type=jnp.float32).astype(jnp.bfloat16)
    proc_target = jnp.dot(mesh_mid, proc_receiver, preferred_element_type=jnp.float32)
    proc_sum = edge_sums(proc_message, proc_target, proc_source).astype(jnp.bfloat16)
    mesh_out = (mesh_mid.astype(jnp.float32) + jnp.dot(proc_sum, proc_update, preferred_element_type=jnp.float32)).astype(jnp.bfloat16)

    grad_proc_update = transpose_dot(proc_sum, cotangent)
    grad_proc_sum = dot_transposed(cotangent, proc_update)
    proc_target_grad, proc_message_grad = edge_grads(proc_message, proc_target, proc_source, grad_proc_sum)
    proc_target_grad = proc_target_grad.astype(jnp.bfloat16)
    proc_message_grad = proc_message_grad.astype(jnp.bfloat16)
    grad_proc_sender = transpose_dot(mesh_mid, proc_message_grad)
    grad_proc_receiver = transpose_dot(mesh_mid, proc_target_grad)
    mid_grad = (cotangent.astype(jnp.float32) + dot_transposed(proc_message_grad, proc_sender) + dot_transposed(proc_target_grad, proc_receiver)).astype(jnp.bfloat16)
    grad_enc_update = transpose_dot(enc_sum, mid_grad)
    grad_enc_sum = dot_transposed(mid_grad, enc_update)
    enc_target_grad, enc_message_grad = edge_grads(enc_message, enc_target, enc_source, grad_enc_sum)
    enc_target_grad = enc_target_grad.astype(jnp.bfloat16)
    enc_message_grad = enc_message_grad.astype(jnp.bfloat16)
    grad_enc_receiver = transpose_dot(mesh_input, enc_target_grad)
    grad_enc_sender = transpose_dot(grid_latent, enc_message_grad)
    pre_grid_grad = (dot_transposed(enc_message_grad, enc_sender) * silu_slope(pre_grid)).astype(jnp.bfloat16)
    grad_embed = transpose_dot(grid_input, pre_grid_grad)
    return (mesh_out, grad_embed, grad_enc_sender, grad_enc_receiver, grad_enc_update, grad_proc_sender, grad_proc_receiver, grad_proc_update)
```

```python
import jax
import jax.numpy as jnp
from jax import lax
from jax.experimental import pallas as pl
from jax.experimental.pallas import tpu as pltpu
from jax.sharding import PartitionSpec as P

lat_steps = (-1, -1, -1, 0, 0, 1, 1, 1)
lon_steps = (-1, 0, 1, -1, 1, -1, 0, 1)
MESH = pl.DeviceIdType.MESH
BLOCK = 512


def neighbour(code):
    lat_count = lax.axis_size("lat")
    lon_count = lax.axis_size("lon")
    lat = lax.axis_index("lat") + lat_steps[code]
    lon = lax.rem(lax.axis_index("lon") + lon_steps[code] + lon_count, lon_count)
    return (lat, lon), (lat >= 0) & (lat < lat_count)


def greet():
    barrier = pltpu.get_barrier_semaphore()
    for code in range(8):
        device, present = neighbour(code)

        @pl.when(present)
        def _():
            pl.semaphore_signal(barrier, inc=1, device_id=device, device_id_type=MESH)


def await_greetings():
    lat = lax.axis_index("lat")
    last = lax.axis_size("lat") - 1
    peers = 2 + 3 * jnp.minimum(lat, 1) + 3 * jnp.minimum(last - lat, 1)
    pl.semaphore_wait(pltpu.get_barrier_semaphore(), peers)


def block_copy(code, land, outgoing, arrived, send_sem, recv_sem):
    cap = outgoing.shape[0] // 8
    device, present = neighbour(code)
    copy = pltpu.make_async_remote_copy(
        src_ref=outgoing.at[pl.ds(code * cap, cap)],
        dst_ref=arrived.at[pl.ds(land * cap, cap)],
        send_sem=send_sem.at[code],
        recv_sem=recv_sem.at[land],
        device_id=device,
        device_id_type=MESH,
    )
    return copy, present


def send_blocks(outgoing, arrived, send_sem, recv_sem):
    cap = outgoing.shape[0] // 8
    for code in range(8):
        copy, present = block_copy(code, 7 - code, outgoing, arrived, send_sem, recv_sem)

        @pl.when(present)
        def _():
            copy.start()

        @pl.when(jnp.logical_not(present))
        def _():
            arrived[pl.ds(code * cap, cap)] = jnp.zeros((cap, arrived.shape[1]), arrived.dtype)


def await_blocks(outgoing, arrived, send_sem, recv_sem):
    for code in range(8):
        copy, present = block_copy(code, code, outgoing, arrived, send_sem, recv_sem)

        @pl.when(present)
        def _():
            copy.wait_send()
            copy.wait_recv()


def pick(column, width, first=0):
    lanes = lax.broadcasted_iota(jnp.int32, (column.shape[0], width), 1) + first
    return jnp.where(column == lanes, 1.0, 0.0).astype(jnp.bfloat16)


def place(row, height, first):
    sublanes = lax.broadcasted_iota(jnp.int32, (height, row.shape[1]), 0) + first
    return jnp.where(row == sublanes, 1.0, 0.0).astype(jnp.bfloat16)


def matmul(left, right):
    return jnp.dot(left, right, preferred_element_type=jnp.float32)


def forward_kernel(
    rows, slots, edges, target, sums, slope, outgoing, arrived, send_sem, recv_sem
):
    own = rows.shape[0]
    fan, count, width = slope.shape
    slot_count = outgoing.shape[0]
    greet()
    outgoing[...] = matmul(pick(slots[...], own), rows[...]).astype(jnp.bfloat16)
    await_greetings()
    send_blocks(outgoing, arrived, send_sem, recv_sem)

    @pl.loop(0, count // BLOCK)
    def _(step):
        here = pl.ds(pl.multiple_of(step * BLOCK, BLOCK), BLOCK)
        for k in range(fan):
            slope[k, here] = matmul(pick(edges[here, k : k + 1], own), rows[...]).astype(
                jnp.bfloat16
            )

    await_blocks(outgoing, arrived, send_sem, recv_sem)
    half = BLOCK // 2

    @pl.loop(0, count // half)
    def _(step):
        here = pl.ds(pl.multiple_of(step * half, half), half)
        total = jnp.zeros((half, width), jnp.float32)
        for k in range(fan):
            far = matmul(pick(edges[here, k : k + 1], slot_count, own), arrived[...])
            before = slope[k, here].astype(jnp.float32) + far + target[here]
            sigmoid = 0.5 * jnp.tanh(0.5 * before) + 0.5
            total = total + before * sigmoid
            slope[k, here] = (sigmoid * (1.0 + before * (1.0 - sigmoid))).astype(jnp.bfloat16)
        sums[here] = total.astype(jnp.bfloat16)


def backward_kernel(
    slope, grad, edges, slots, target_grad, message_grad, edge_grad, local, outgoing, arrived, send_sem, recv_sem
):
    own = message_grad.shape[0]
    fan, count, width = slope.shape
    slot_count = outgoing.shape[0]
    half = BLOCK // 2
    greet()

    @pl.loop(0, count // half)
    def _(step):
        first = pl.multiple_of(step * half, half)
        here = pl.ds(first, half)
        total = jnp.zeros((half, width), jnp.float32)
        for k in range(fan):
            one = grad[here] * slope[k, here].astype(jnp.float32)
            total = total + one
            edge_grad[pl.ds(pl.multiple_of(k * count + first, half), half)] = one.astype(jnp.bfloat16)
        target_grad[here] = total.astype(jnp.bfloat16)

    outgoing[...] = matmul(place(edges[...], slot_count, own), edge_grad[...]).astype(jnp.bfloat16)
    await_greetings()
    send_blocks(outgoing, arrived, send_sem, recv_sem)

    @pl.loop(0, own // BLOCK)
    def _(step):
        first = pl.multiple_of(step * BLOCK, BLOCK)
        local[pl.ds(first, BLOCK)] = matmul(place(edges[...], BLOCK, first), edge_grad[...])

    await_blocks(outgoing, arrived, send_sem, recv_sem)

    @pl.loop(0, own // BLOCK)
    def _(step):
        first = pl.multiple_of(step * BLOCK, BLOCK)
        here = pl.ds(first, BLOCK)
        far = matmul(place(slots[...], BLOCK, first), arrived[...])
        message_grad[here] = (local[here] + far).astype(jnp.bfloat16)


def halo_scratch(slot_count, width):
    return [
        pltpu.VMEM((slot_count, width), jnp.bfloat16),
        pltpu.VMEM((slot_count, width), jnp.bfloat16),
        pltpu.SemaphoreType.DMA((8,)),
        pltpu.SemaphoreType.DMA((8,)),
    ]


def edge_forward(rows, slots, edges, target, number):
    own, width = rows.shape
    fan, count = edges.shape
    slot_count = slots.shape[0]
    vmem = pl.BlockSpec(memory_space=pltpu.VMEM)
    return pl.pallas_call(
        forward_kernel,
        out_shape=(
            jax.ShapeDtypeStruct((count, width), jnp.bfloat16),
            jax.ShapeDtypeStruct((fan, count, width), jnp.bfloat16),
        ),
        in_specs=[vmem] * 4,
        out_specs=(vmem, vmem),
        scratch_shapes=halo_scratch(slot_count, width),
        compiler_params=pltpu.CompilerParams(
            collective_id=number, has_side_effects=True, vmem_limit_bytes=50 * 2**20
        ),
        cost_estimate=pl.CostEstimate(
            flops=2 * fan * count * (own + slot_count) * width,
            bytes_accessed=12 * count * width,
            transcendentals=fan * count * width,
        ),
    )(rows, slots.reshape(-1, 1), edges.T, target)


def edge_backward(slope, grad, edges, slots, own, number):
    fan, count, width = slope.shape
    slot_count = slots.shape[0]
    vmem = pl.BlockSpec(memory_space=pltpu.VMEM)
    return pl.pallas_call(
        backward_kernel,
        out_shape=(
            jax.ShapeDtypeStruct((count, width), jnp.bfloat16),
            jax.ShapeDtypeStruct((own, width), jnp.bfloat16),
        ),
        in_specs=[vmem] * 4,
        out_specs=(vmem, vmem),
        scratch_shapes=[
            pltpu.VMEM((fan * count, width), jnp.bfloat16),
            pltpu.VMEM((own, width), jnp.float32),
        ]
        + halo_scratch(slot_count, width),
        compiler_params=pltpu.CompilerParams(
            collective_id=number, has_side_effects=True, vmem_limit_bytes=50 * 2**20
        ),
        cost_estimate=pl.CostEstimate(
            flops=2 * fan * count * (own + slot_count) * width,
            bytes_accessed=12 * count * width,
            transcendentals=0,
        ),
    )(slope, grad, edges.reshape(1, -1), slots.reshape(1, -1))


def silu_slope(values):
    sigmoid = jax.nn.sigmoid(values)
    return sigmoid * (1.0 + values * (1.0 - sigmoid))


def transpose_dot(left, right):
    return lax.dot_general(
        left, right, (((0,), (0,)), ((), ())), preferred_element_type=jnp.float32
    )


def dot_transposed(left, right):
    return lax.dot_general(
        left, right, (((1,), (1,)), ((), ())), preferred_element_type=jnp.float32
    )


def local(
    grid_input,
    mesh_input,
    cotangent,
    embed_weight,
    enc_sender,
    enc_receiver,
    enc_update,
    proc_sender,
    proc_receiver,
    proc_update,
    grid_slots,
    enc_edges,
    mesh_slots,
    mesh_edges,
):
    grid_count = grid_input.shape[0]
    mesh_count = mesh_input.shape[0]
    pre_grid = jnp.dot(grid_input, embed_weight, preferred_element_type=jnp.float32)
    grid_latent = jax.nn.silu(pre_grid).astype(jnp.bfloat16)
    enc_message = jnp.dot(grid_latent, enc_sender, preferred_element_type=jnp.float32).astype(
        jnp.bfloat16
    )
    enc_target = jnp.dot(mesh_input, enc_receiver, preferred_element_type=jnp.float32)
    enc_sum, enc_slope = edge_forward(enc_message, grid_slots, enc_edges, enc_target, 0)
    mesh_mid = (
        mesh_input.astype(jnp.float32)
        + jnp.dot(enc_sum, enc_update, preferred_element_type=jnp.float32)
    ).astype(jnp.bfloat16)
    proc_message = jnp.dot(mesh_mid, proc_sender, preferred_element_type=jnp.float32).astype(
        jnp.bfloat16
    )
    proc_target = jnp.dot(mesh_mid, proc_receiver, preferred_element_type=jnp.float32)
    proc_sum, proc_slope = edge_forward(proc_message, mesh_slots, mesh_edges, proc_target, 1)
    mesh_out = (
        mesh_mid.astype(jnp.float32)
        + jnp.dot(proc_sum, proc_update, preferred_element_type=jnp.float32)
    ).astype(jnp.bfloat16)
    grad_proc_update = transpose_dot(proc_sum, cotangent)
    grad_proc_sum = dot_transposed(cotangent, proc_update)
    proc_target_grad, proc_message_grad = edge_backward(
        proc_slope, grad_proc_sum, mesh_edges, mesh_slots, mesh_count, 2
    )
    grad_proc_sender = transpose_dot(mesh_mid, proc_message_grad)
    grad_proc_receiver = transpose_dot(mesh_mid, proc_target_grad)
    mid_grad = (
        cotangent.astype(jnp.float32)
        + dot_transposed(proc_message_grad, proc_sender)
        + dot_transposed(proc_target_grad, proc_receiver)
    ).astype(jnp.bfloat16)
    grad_enc_update = transpose_dot(enc_sum, mid_grad)
    grad_enc_sum = dot_transposed(mid_grad, enc_update)
    early = lax.psum(
        jnp.stack([grad_proc_update, grad_proc_sender, grad_proc_receiver, grad_enc_update]).astype(
            jnp.bfloat16
        ),
        ("lat", "lon"),
    )
    enc_target_grad, enc_message_grad = edge_backward(
        enc_slope, grad_enc_sum, enc_edges, grid_slots, grid_count, 3
    )
    grad_enc_receiver = transpose_dot(mesh_input, enc_target_grad)
    grad_enc_sender = transpose_dot(grid_latent, enc_message_grad)
    pre_grid_grad = (dot_transposed(enc_message_grad, enc_sender) * silu_slope(pre_grid)).astype(
        jnp.bfloat16
    )
    grad_embed = transpose_dot(grid_input, pre_grid_grad)
    late = jnp.concatenate([grad_enc_sender, grad_enc_receiver, grad_embed]).astype(jnp.bfloat16)
    late, early = lax.optimization_barrier((late, early))
    late = lax.psum(late, ("lat", "lon")).astype(jnp.float32)
    early = early.astype(jnp.float32)
    latent_width = enc_sender.shape[0]
    grad_enc_sender = late[:latent_width]
    grad_enc_receiver = late[latent_width : 2 * latent_width]
    grad_embed = late[2 * latent_width :]
    grad_proc_update, grad_proc_sender, grad_proc_receiver, grad_enc_update = early
    return (
        mesh_out,
        grad_embed,
        grad_enc_sender,
        grad_enc_receiver,
        grad_enc_update,
        grad_proc_sender,
        grad_proc_receiver,
        grad_proc_update,
    )


def solution(mesh):
    placed = (
        P(("lat", "lon"), None),
        P(("lat", "lon"), None),
        P(("lat", "lon"), None),
        P(),
        P(),
        P(),
        P(),
        P(),
        P(),
        P(),
        P(("lat", "lon")),
        P(None, ("lat", "lon")),
        P(("lat", "lon")),
        P(None, ("lat", "lon")),
    )
    return jax.shard_map(
        local,
        mesh=mesh,
        in_specs=placed,
        out_specs=(P(("lat", "lon"), None), P(), P(), P(), P(), P(), P(), P()),
        check_vma=False,
    )
```

```python
import functools

import jax
import jax.numpy as jnp
from jax import lax
from jax.experimental import pallas as pl
from jax.experimental.pallas import tpu as pltpu
from jax.sharding import PartitionSpec as P

lat_steps = (-1, -1, -1, 0, 0, 1, 1, 1)
lon_steps = (-1, 0, 1, -1, 1, -1, 0, 1)
MESH = pl.DeviceIdType.MESH
BLOCK = 512


def neighbour(code):
    lat_count = lax.axis_size("lat")
    lon_count = lax.axis_size("lon")
    lat = lax.axis_index("lat") + lat_steps[code]
    lon = lax.rem(lax.axis_index("lon") + lon_steps[code] + lon_count, lon_count)
    return (lat, lon), (lat >= 0) & (lat < lat_count)


def greet():
    barrier = pltpu.get_barrier_semaphore()
    for code in range(8):
        device, present = neighbour(code)

        @pl.when(present)
        def _():
            pl.semaphore_signal(barrier, inc=1, device_id=device, device_id_type=MESH)


def await_greetings(others=0):
    lat = lax.axis_index("lat")
    last = lax.axis_size("lat") - 1
    peers = 2 + 3 * jnp.minimum(lat, 1) + 3 * jnp.minimum(last - lat, 1) + others
    pl.semaphore_wait(pltpu.get_barrier_semaphore(), peers)


def block_copy(code, land, outgoing, arrived, send_sem, recv_sem):
    cap = outgoing.shape[0] // 8
    device, present = neighbour(code)
    copy = pltpu.make_async_remote_copy(
        src_ref=outgoing.at[pl.ds(code * cap, cap)],
        dst_ref=arrived.at[pl.ds(land * cap, cap)],
        send_sem=send_sem.at[code],
        recv_sem=recv_sem.at[land],
        device_id=device,
        device_id_type=MESH,
    )
    return copy, present


def send_blocks(outgoing, arrived, send_sem, recv_sem):
    cap = outgoing.shape[0] // 8
    for code in range(8):
        copy, present = block_copy(code, 7 - code, outgoing, arrived, send_sem, recv_sem)

        @pl.when(present)
        def _():
            copy.start()

        @pl.when(jnp.logical_not(present))
        def _():
            arrived[pl.ds(code * cap, cap)] = jnp.zeros((cap, arrived.shape[1]), arrived.dtype)


def await_blocks(outgoing, arrived, send_sem, recv_sem):
    for code in range(8):
        copy, present = block_copy(code, code, outgoing, arrived, send_sem, recv_sem)

        @pl.when(present)
        def _():
            copy.wait_send()
            copy.wait_recv()


def pick(column, width, first=0):
    lanes = lax.broadcasted_iota(jnp.int32, (column.shape[0], width), 1) + first
    return jnp.where(column == lanes, 1.0, 0.0).astype(jnp.bfloat16)


def place(row, height, first):
    sublanes = lax.broadcasted_iota(jnp.int32, (height, row.shape[1]), 0) + first
    return jnp.where(row == sublanes, 1.0, 0.0).astype(jnp.bfloat16)


def matmul(left, right):
    return jnp.dot(left, right, preferred_element_type=jnp.float32)


class Reduction:
    def __init__(self, value, result, lands, works, send_sem, recv_sem):
        self.value, self.result, self.lands, self.works = value, result, lands, works
        self.send_sem, self.recv_sem = send_sem, recv_sem
        self.phases, self.rows = reduction_plan(
            value.shape[0], lax.axis_size("lat"), lax.axis_size("lon")
        )

    def spot(self, phase):
        axis, stride, size = self.phases[phase]
        return lax.rem(lax.axis_index(axis) // stride, size)

    def device(self, phase, distance):
        axis, stride, size = self.phases[phase]
        spot = self.spot(phase)
        other = lax.rem(spot + distance, size)
        index = lax.axis_index(axis) + (other - spot) * stride
        if axis == "lat":
            return other, (index, lax.axis_index("lon"))
        return other, (lax.axis_index("lat"), index)

    def offset(self, phase):
        return sum(self.spot(p) * self.rows[p + 1] for p in range(phase))

    def peers(self):
        return sum(size - 1 for _, _, size in self.phases)

    def greet(self):
        barrier = pltpu.get_barrier_semaphore()
        for phase, (_, _, size) in enumerate(self.phases):
            for distance in range(1, size):
                _, device = self.device(phase, distance)
                pl.semaphore_signal(barrier, inc=1, device_id=device, device_id_type=MESH)

    def semaphore(self, phase, distance, gathering):
        before = sum(size - 1 for _, _, size in self.phases[:phase])
        return gathering * self.peers() + before + distance - 1

    def scatter_copy(self, phase, distance):
        other, device = self.device(phase, distance)
        source = self.works[phase - 1] if phase else self.value
        part = self.rows[phase + 1]
        at = self.semaphore(phase, distance, 0)
        return pltpu.make_async_remote_copy(
            src_ref=source.at[pl.ds(pl.multiple_of(other * part, 16), part)],
            dst_ref=self.lands[phase].at[pl.ds((distance - 1) * part, part)],
            send_sem=self.send_sem.at[at],
            recv_sem=self.recv_sem.at[at],
            device_id=device,
            device_id_type=MESH,
        )

    def gather_copy(self, phase, distance, arriving):
        _, stride, size = self.phases[phase]
        _, device = self.device(phase, distance)
        part = self.rows[phase + 1]
        own = self.offset(phase + 1)
        spot = self.spot(phase)
        sender = lax.rem(spot + size - distance, size)
        land = own + (sender - spot) * part if arriving else own
        at = self.semaphore(phase, distance, 1)
        return pltpu.make_async_remote_copy(
            src_ref=self.result.at[pl.ds(pl.multiple_of(own, 16), part)],
            dst_ref=self.result.at[pl.ds(pl.multiple_of(land, 16), part)],
            send_sem=self.send_sem.at[at],
            recv_sem=self.recv_sem.at[at],
            device_id=device,
            device_id_type=MESH,
        )

    def scatter_start(self, phase):
        for distance in range(1, self.phases[phase][2]):
            self.scatter_copy(phase, distance).start()

    def scatter_finish(self, phase):
        size = self.phases[phase][2]
        part = self.rows[phase + 1]
        for distance in range(1, size):
            self.scatter_copy(phase, distance).wait()
        source = self.works[phase - 1] if phase else self.value
        total = source[pl.ds(pl.multiple_of(self.spot(phase) * part, 16), part)].astype(jnp.float32)
        for distance in range(1, size):
            total = total + self.lands[phase][pl.ds((distance - 1) * part, part)].astype(
                jnp.float32
            )
        total = total.astype(jnp.bfloat16)
        if phase + 1 < len(self.phases):
            self.works[phase][...] = total
        else:
            self.result[pl.ds(pl.multiple_of(self.offset(phase + 1), 16), part)] = total

    def gather_start(self, phase):
        for distance in range(1, self.phases[phase][2]):
            self.gather_copy(phase, distance, False).start()

    def gather_finish(self, phase):
        for distance in range(1, self.phases[phase][2]):
            self.gather_copy(phase, distance, False).wait_send()
            self.gather_copy(phase, distance, True).wait_recv()


def reduction_plan(row_count, lat_count, lon_count):
    phases = (("lon", 1, 2), ("lon", 2, lon_count // 2), ("lat", 1, lat_count))
    rows = [row_count]
    for _, _, size in phases:
        rows.append(rows[-1] // size)
    return phases, rows


def reduction_scratch(arrays, lat_count, lon_count):
    unit = 16 * lat_count * lon_count
    row_count = -(-2 * sum(a.shape[0] for a in arrays) // unit) * unit
    width = arrays[0].shape[1] // 2
    phases, rows = reduction_plan(row_count, lat_count, lon_count)
    lands = [
        pltpu.VMEM(((size - 1) * part, width), jnp.bfloat16)
        for (_, _, size), part in zip(phases, rows[1:])
    ]
    works = [pltpu.VMEM((part, width), jnp.bfloat16) for part in rows[1:-1]]
    semaphores = 2 * sum(size - 1 for _, _, size in phases)
    whole = pltpu.VMEM((row_count, width), jnp.bfloat16)
    return [whole, whole] + lands + works + [pltpu.SemaphoreType.DMA((semaphores,))] * 2


def reduction_of(scratch):
    value, result, land0, land1, land2, work0, work1, send_sem, recv_sem = scratch
    return Reduction(value, result, (land0, land1, land2), (work0, work1), send_sem, recv_sem)


def pack(arrays, value):
    first = 0
    for array in arrays:
        height, width = array.shape[0], array.shape[1] // 2
        value[pl.ds(first, height)] = array[:, :width]
        value[pl.ds(first + height, height)] = array[:, width:]
        first += 2 * height
    if first < value.shape[0]:
        value[pl.ds(first, value.shape[0] - first)] = jnp.zeros(
            (value.shape[0] - first, value.shape[1]), value.dtype
        )


def unpack(result, outputs):
    first = 0
    for output in outputs:
        height, width = output.shape[0], output.shape[1] // 2
        output[:, :width] = result[pl.ds(first, height)]
        output[:, width:] = result[pl.ds(first + height, height)]
        first += 2 * height


def reduce_kernel(number, *refs):
    inputs, outputs = refs[:number], refs[number : 2 * number]
    reduction = reduction_of(refs[2 * number :])
    reduction.greet()
    pack(inputs, reduction.value)
    pl.semaphore_wait(pltpu.get_barrier_semaphore(), reduction.peers())
    for phase in (0, 1, 2):
        reduction.scatter_start(phase)
        reduction.scatter_finish(phase)
    for phase in (2, 1, 0):
        reduction.gather_start(phase)
        reduction.gather_finish(phase)
    unpack(reduction.result, outputs)


def reduce_all(arrays, number):
    vmem = pl.BlockSpec(memory_space=pltpu.VMEM)
    return pl.pallas_call(
        functools.partial(reduce_kernel, len(arrays)),
        out_shape=tuple(jax.ShapeDtypeStruct(a.shape, a.dtype) for a in arrays),
        in_specs=[vmem] * len(arrays),
        out_specs=(vmem,) * len(arrays),
        scratch_shapes=reduction_scratch(arrays, lax.axis_size("lat"), lax.axis_size("lon")),
        compiler_params=pltpu.CompilerParams(
            collective_id=number, has_side_effects=True, vmem_limit_bytes=50 * 2**20
        ),
    )(*arrays)


def forward_kernel(
    rows, slots, edges, target, sums, slope, outgoing, arrived, send_sem, recv_sem
):
    own = rows.shape[0]
    fan, count, width = slope.shape
    slot_count = outgoing.shape[0]
    greet()
    outgoing[...] = matmul(pick(slots[...], own), rows[...]).astype(jnp.bfloat16)
    await_greetings()
    send_blocks(outgoing, arrived, send_sem, recv_sem)

    @pl.loop(0, count // BLOCK)
    def _(step):
        here = pl.ds(pl.multiple_of(step * BLOCK, BLOCK), BLOCK)
        for k in range(fan):
            slope[k, here] = matmul(pick(edges[here, k : k + 1], own), rows[...]).astype(
                jnp.bfloat16
            )

    await_blocks(outgoing, arrived, send_sem, recv_sem)
    half = BLOCK // 2

    @pl.loop(0, count // half)
    def _(step):
        here = pl.ds(pl.multiple_of(step * half, half), half)
        total = jnp.zeros((half, width), jnp.float32)
        for k in range(fan):
            far = matmul(pick(edges[here, k : k + 1], slot_count, own), arrived[...])
            before = slope[k, here].astype(jnp.float32) + far + target[here]
            sigmoid = 0.5 * jnp.tanh(0.5 * before) + 0.5
            total = total + before * sigmoid
            slope[k, here] = (sigmoid * (1.0 + before * (1.0 - sigmoid))).astype(jnp.bfloat16)
        sums[here] = total.astype(jnp.bfloat16)


def backward_kernel(early_count, slope, grad, edges, slots, *refs):
    early, refs = refs[:early_count], refs[early_count:]
    target_grad, message_grad, refs = refs[0], refs[1], refs[2:]
    early_sums, refs = refs[:early_count], refs[early_count:]
    edge_grad, local, outgoing, arrived, send_sem, recv_sem = refs[:6]
    reduction = reduction_of(refs[6:]) if early_count else None
    own = message_grad.shape[0]
    fan, count, width = slope.shape
    slot_count = outgoing.shape[0]
    half = BLOCK // 2
    greet()
    if reduction:
        reduction.greet()
        pack(early, reduction.value)
        await_greetings(reduction.peers())
        reduction.scatter_start(0)

    @pl.loop(0, count // half)
    def _(step):
        first = pl.multiple_of(step * half, half)
        here = pl.ds(first, half)
        total = jnp.zeros((half, width), jnp.float32)
        for k in range(fan):
            one = grad[here] * slope[k, here].astype(jnp.float32)
            total = total + one
            edge_grad[pl.ds(pl.multiple_of(k * count + first, half), half)] = one.astype(
                jnp.bfloat16
            )
        target_grad[here] = total.astype(jnp.bfloat16)

    outgoing[...] = matmul(place(edges[...], slot_count, own), edge_grad[...]).astype(jnp.bfloat16)
    if not reduction:
        await_greetings()
    send_blocks(outgoing, arrived, send_sem, recv_sem)
    if reduction:
        reduction.scatter_finish(0)
        reduction.scatter_start(1)

    def spread(begin, end):
        @pl.loop(begin, end)
        def _(step):
            first = pl.multiple_of(step * BLOCK, BLOCK)
            local[pl.ds(first, BLOCK)] = matmul(place(edges[...], BLOCK, first), edge_grad[...])

    steps = own // BLOCK
    if reduction:
        spread(0, steps * 3 // 4)
        reduction.scatter_finish(1)
        reduction.scatter_start(2)
        spread(steps * 3 // 4, steps)
        reduction.scatter_finish(2)
        reduction.gather_start(2)
    else:
        spread(0, steps)

    await_blocks(outgoing, arrived, send_sem, recv_sem)

    @pl.loop(0, own // BLOCK)
    def _(step):
        first = pl.multiple_of(step * BLOCK, BLOCK)
        here = pl.ds(first, BLOCK)
        far = matmul(place(slots[...], BLOCK, first), arrived[...])
        message_grad[here] = (local[here] + far).astype(jnp.bfloat16)

    if reduction:
        reduction.gather_finish(2)
        for phase in (1, 0):
            reduction.gather_start(phase)
            reduction.gather_finish(phase)
        unpack(reduction.result, early_sums)


def halo_scratch(slot_count, width):
    return [
        pltpu.VMEM((slot_count, width), jnp.bfloat16),
        pltpu.VMEM((slot_count, width), jnp.bfloat16),
        pltpu.SemaphoreType.DMA((8,)),
        pltpu.SemaphoreType.DMA((8,)),
    ]


def edge_forward(rows, slots, edges, target, number):
    own, width = rows.shape
    fan, count = edges.shape
    slot_count = slots.shape[0]
    vmem = pl.BlockSpec(memory_space=pltpu.VMEM)
    return pl.pallas_call(
        forward_kernel,
        out_shape=(
            jax.ShapeDtypeStruct((count, width), jnp.bfloat16),
            jax.ShapeDtypeStruct((fan, count, width), jnp.bfloat16),
        ),
        in_specs=[vmem] * 4,
        out_specs=(vmem, vmem),
        scratch_shapes=halo_scratch(slot_count, width),
        compiler_params=pltpu.CompilerParams(
            collective_id=number, has_side_effects=True, vmem_limit_bytes=50 * 2**20
        ),
        cost_estimate=pl.CostEstimate(
            flops=2 * fan * count * (own + slot_count) * width,
            bytes_accessed=12 * count * width,
            transcendentals=fan * count * width,
        ),
    )(rows, slots.reshape(-1, 1), edges.T, target)


def edge_backward(slope, grad, edges, slots, own, number, early=()):
    fan, count, width = slope.shape
    slot_count = slots.shape[0]
    scratch = []
    if early:
        scratch = reduction_scratch(early, lax.axis_size("lat"), lax.axis_size("lon"))
    vmem = pl.BlockSpec(memory_space=pltpu.VMEM)
    return pl.pallas_call(
        functools.partial(backward_kernel, len(early)),
        out_shape=(
            jax.ShapeDtypeStruct((count, width), jnp.bfloat16),
            jax.ShapeDtypeStruct((own, width), jnp.bfloat16),
        )
        + tuple(jax.ShapeDtypeStruct(a.shape, a.dtype) for a in early),
        in_specs=[vmem] * (4 + len(early)),
        out_specs=(vmem,) * (2 + len(early)),
        scratch_shapes=[
            pltpu.VMEM((fan * count, width), jnp.bfloat16),
            pltpu.VMEM((own, width), jnp.float32),
        ]
        + halo_scratch(slot_count, width)
        + scratch,
        compiler_params=pltpu.CompilerParams(
            collective_id=number, has_side_effects=True, vmem_limit_bytes=50 * 2**20
        ),
        cost_estimate=pl.CostEstimate(
            flops=2 * fan * count * (own + slot_count) * width,
            bytes_accessed=12 * count * width,
            transcendentals=0,
        ),
    )(slope, grad, edges.reshape(1, -1), slots.reshape(1, -1), *early)


def silu_slope(values):
    sigmoid = jax.nn.sigmoid(values)
    return sigmoid * (1.0 + values * (1.0 - sigmoid))


def transpose_dot(left, right):
    return lax.dot_general(
        left, right, (((0,), (0,)), ((), ())), preferred_element_type=jnp.float32
    )


def dot_transposed(left, right):
    return lax.dot_general(
        left, right, (((1,), (1,)), ((), ())), preferred_element_type=jnp.float32
    )


def local(
    grid_input,
    mesh_input,
    cotangent,
    embed_weight,
    enc_sender,
    enc_receiver,
    enc_update,
    proc_sender,
    proc_receiver,
    proc_update,
    grid_slots,
    enc_edges,
    mesh_slots,
    mesh_edges,
):
    grid_count = grid_input.shape[0]
    mesh_count = mesh_input.shape[0]
    pre_grid = jnp.dot(grid_input, embed_weight, preferred_element_type=jnp.float32)
    grid_latent = jax.nn.silu(pre_grid).astype(jnp.bfloat16)
    enc_message = jnp.dot(grid_latent, enc_sender, preferred_element_type=jnp.float32).astype(
        jnp.bfloat16
    )
    enc_target = jnp.dot(mesh_input, enc_receiver, preferred_element_type=jnp.float32)
    enc_sum, enc_slope = edge_forward(enc_message, grid_slots, enc_edges, enc_target, 0)
    mesh_mid = (
        mesh_input.astype(jnp.float32)
        + jnp.dot(enc_sum, enc_update, preferred_element_type=jnp.float32)
    ).astype(jnp.bfloat16)
    proc_message = jnp.dot(mesh_mid, proc_sender, preferred_element_type=jnp.float32).astype(
        jnp.bfloat16
    )
    proc_target = jnp.dot(mesh_mid, proc_receiver, preferred_element_type=jnp.float32)
    proc_sum, proc_slope = edge_forward(proc_message, mesh_slots, mesh_edges, proc_target, 1)
    mesh_out = (
        mesh_mid.astype(jnp.float32)
        + jnp.dot(proc_sum, proc_update, preferred_element_type=jnp.float32)
    ).astype(jnp.bfloat16)
    grad_proc_update = transpose_dot(proc_sum, cotangent)
    grad_proc_sum = dot_transposed(cotangent, proc_update)
    proc_target_grad, proc_message_grad = edge_backward(
        proc_slope, grad_proc_sum, mesh_edges, mesh_slots, mesh_count, 2
    )
    grad_proc_sender = transpose_dot(mesh_mid, proc_message_grad)
    grad_proc_receiver = transpose_dot(mesh_mid, proc_target_grad)
    mid_grad = (
        cotangent.astype(jnp.float32)
        + dot_transposed(proc_message_grad, proc_sender)
        + dot_transposed(proc_target_grad, proc_receiver)
    ).astype(jnp.bfloat16)
    grad_enc_update = transpose_dot(enc_sum, mid_grad)
    grad_enc_sum = dot_transposed(mid_grad, enc_update)
    early = [
        g.astype(jnp.bfloat16)
        for g in (grad_proc_update, grad_proc_sender, grad_proc_receiver, grad_enc_update)
    ]
    enc_target_grad, enc_message_grad, *early = edge_backward(
        enc_slope, grad_enc_sum, enc_edges, grid_slots, grid_count, 3, tuple(early)
    )
    grad_enc_receiver = transpose_dot(mesh_input, enc_target_grad)
    grad_enc_sender = transpose_dot(grid_latent, enc_message_grad)
    pre_grid_grad = (dot_transposed(enc_message_grad, enc_sender) * silu_slope(pre_grid)).astype(
        jnp.bfloat16
    )
    grad_embed = transpose_dot(grid_input, pre_grid_grad)
    features = grad_embed.shape[0]
    grad_embed = jnp.pad(grad_embed, ((0, -features % 256), (0, 0)))
    late = [g.astype(jnp.bfloat16) for g in (grad_enc_sender, grad_enc_receiver, grad_embed)]
    late = [g.astype(jnp.float32) for g in reduce_all(tuple(late), 4)]
    grad_enc_sender, grad_enc_receiver, grad_embed = late
    grad_embed = grad_embed[:features]
    grad_proc_update, grad_proc_sender, grad_proc_receiver, grad_enc_update = [
        g.astype(jnp.float32) for g in early
    ]
    return (
        mesh_out,
        grad_embed,
        grad_enc_sender,
        grad_enc_receiver,
        grad_enc_update,
        grad_proc_sender,
        grad_proc_receiver,
        grad_proc_update,
    )


def solution(mesh):
    placed = (
        P(("lat", "lon"), None),
        P(("lat", "lon"), None),
        P(("lat", "lon"), None),
        P(),
        P(),
        P(),
        P(),
        P(),
        P(),
        P(),
        P(("lat", "lon")),
        P(None, ("lat", "lon")),
        P(("lat", "lon")),
        P(None, ("lat", "lon")),
    )
    return jax.shard_map(
        local,
        mesh=mesh,
        in_specs=placed,
        out_specs=(P(("lat", "lon"), None), P(), P(), P(), P(), P(), P(), P()),
        check_vma=False,
    )
```
